128 devices in a mesh: dp: 16 (over y, x), tensor: 8 (over z, core).
Axes of the slice: x: 4, y: 4, z: 4, core: 2. Of those that a mesh axis runs over, the one named last changes fastest.
Arguments:
- act_codes: int32 [8192, 28672], P('dp', 'tensor'), may hold values from 40 to 199, as said below
- grad_codes: int32 [8192, 4096], P(('dp', 'tensor')), may hold values from 40 to 199, as said below
- amax_history: float32 [128, 1024], P(('dp', 'tensor')), may hold values from 0.001953125 to 96, as said below
Outputs:
- weight_grad: float32 [28672, 4096], P('tensor', 'dp')
- new_history: float32 [128, 1024], P(('dp', 'tensor'))
The draws below stay inside these ranges and needn't reach their ends.
Inputs may be any that keep to these rules, and one draw needn't show every extreme that they name: `act_codes`: each code is 128 s + 8 e + m with a sign bit s of 0 or 1, an exponent field e of 5 to 8 and a mantissa m of 0 to 7. `grad_codes`: each code is 128 s + 8 e + m with a sign bit s of 0 or 1, an exponent field e of 5 to 8 and a mantissa m of 0 to 7. `amax_history`: every entry is a whole number times a power of two; the largest entry of the array is (192) times 1/8, 1/4 or 1/2.
All inputs are finite; a program needn't handle non-finite values.
Results may differ from the reference program's by a relative error of at most 0.0003.
Values may be sent and summed in bfloat16 or wider, within the bound.
No kernel may reach another device: no remote copies, remote signals or barrier semaphores. Data moves between devices by JAX's collectives and lax.ppermute only.
A program may use at most 192 MiB of HBM per device.

```python
import jax
import jax.numpy as jnp
from jax import lax

FF = 28672
PANEL = 4096
TOK_DEV = 512
HIST = 1024
TOKENS = 8192
RANKS = 128
LEVELS = 4
N_DP = 16
N_TENSOR = 8


def make_codes(key, shape):
    sign_key, exponent_key, mantissa_key = jax.random.split(key, 3)
    sign_bit = jax.random.randint(sign_key, shape, 0, 2)
    exponent_field = jax.random.randint(exponent_key, shape, 5, 9)
    mantissa = jax.random.randint(mantissa_key, shape, 0, 8)
    return (sign_bit * 128 + exponent_field * 8 + mantissa).astype(jnp.int32)


def draw_act_codes(key, part):
    key = jax.random.fold_in(key, 1)
    return make_codes(key, (TOKENS, FF))


def draw_grad_codes(key, part):
    key = jax.random.fold_in(key, 2)
    return make_codes(key, (TOKENS, PANEL))


def draw_amax_history(key, part):
    key = jax.random.fold_in(key, 3)
    subkeys = jax.random.split(key, 5)
    integers = jax.random.randint(subkeys[0], (RANKS, HIST), 1, 128).astype(jnp.float32)
    shift_index = jax.random.randint(subkeys[1], (RANKS, HIST), 0, 4)
    powers = jnp.array([2.0 ** (-9), 2.0 ** (-8), 2.0 ** (-7), 2.0 ** (-6)], jnp.float32)
    drawn = integers * powers[shift_index]
    top_index = jax.random.randint(subkeys[2], (), 0, 3)
    top_value = (TOK_DEV // 4 + 64) * jnp.array([0.125, 0.25, 0.5], jnp.float32)[top_index]
    row_pick = jax.random.randint(subkeys[3], (), 0, RANKS)
    column_pick = jax.random.randint(subkeys[4], (), 0, HIST)
    row_index = jnp.arange(RANKS)[:, None]
    column_index = jnp.arange(HIST)[None, :]
    chosen = (row_index == row_pick) & (column_index == column_pick)
    return jnp.where(chosen, top_value, drawn).astype(jnp.float32)


def setup_inputs(seed: int = 0) -> dict:
    keys = jax.random.split(jax.random.key(seed), 4)
    act_codes = draw_act_codes(jax.random.fold_in(keys[3], 71), 0)
    grad_codes = draw_grad_codes(jax.random.fold_in(keys[3], 71), 0)
    amax_history = draw_amax_history(jax.random.fold_in(keys[3], 71), 0)
    return {"act_codes": act_codes, "grad_codes": grad_codes, "amax_history": amax_history}


def decode(code_array):
    sign_bit = code_array // 128
    remainder = code_array % 128
    exponent_field = remainder // 8
    mantissa = 8 + remainder % 8
    multiplier = jnp.where(exponent_field >= 8, 8, jnp.where(exponent_field == 7, 4, jnp.where(exponent_field == 6, 2, 1)))
    signed = (1 - 2 * sign_bit) * mantissa * multiplier
    return (signed.astype(jnp.float32) * 0.03125).astype(jnp.bfloat16)


def quantize(values):
    magnitude = jnp.abs(values)
    step_size = jnp.full_like(values, 2.0 ** -9)
    for exponent in range(-5, 9):
        step_size = jnp.where(magnitude >= 2.0 ** exponent, step_size * 2.0, step_size)
    grid_value = jnp.minimum(jnp.floor(magnitude / step_size + 0.5) * step_size, 448.0)
    return jnp.sign(values) * grid_value


def scale_pair(peak):
    scale = peak * 0.0 + 2.0 ** 24
    inverse = peak * 0.0 + 2.0 ** -24
    for exponent in range(-16, 24):
        above = peak > 2.0 ** exponent
        scale = jnp.where(above, scale * 0.5, scale)
        inverse = jnp.where(above, inverse * 2.0, inverse)
    return scale, inverse


def reference(act_codes, grad_codes, amax_history):
    scale, inverse = scale_pair(jnp.max(amax_history))
    output_grad = decode(grad_codes).reshape(N_DP, TOK_DEV, PANEL).astype(jnp.float32)
    block_rows = FF // (4 * N_TENSOR)

    def one_block(index):
        code_block = lax.dynamic_slice_in_dim(act_codes, index * block_rows, block_rows, 1)
        activations = decode(code_block).reshape(N_DP, TOK_DEV, block_rows).astype(jnp.float32)
        partial_value = jnp.einsum("rtf,rtd->rfd", activations, output_grad, precision=lax.Precision.HIGHEST)
        block_peak = jnp.max(jnp.abs(partial_value), axis=(1, 2))
        level = quantize(partial_value * scale).astype(jnp.bfloat16)
        for section in range(LEVELS):
            half = level.shape[0] // 2
            total = level[:half].astype(jnp.float32) + level[half:].astype(jnp.float32)
            level = quantize(total * 0.5).astype(jnp.bfloat16)
        return level[0].astype(jnp.float32) * inverse, block_peak

    indices = jnp.arange(4 * N_TENSOR, dtype=jnp.int32)
    blocks, peaks = lax.map(one_block, indices)
    weight_grad = blocks.reshape(FF, PANEL)
    current_amax = jnp.max(peaks.reshape(N_TENSOR, 4, N_DP), axis=1).T.reshape(RANKS)
    new_history = jnp.concatenate([current_amax[:, None], amax_history[:, :-1]], axis=1)
    return weight_grad, new_history
```

```python
import functools

import jax
import jax.numpy as jnp
from jax import lax
from jax.experimental import pallas as pl
from jax.experimental.pallas import tpu as pltpu
from jax.sharding import PartitionSpec as P

F32 = jnp.float32
BF16 = jnp.bfloat16
NUDGE = 1.0 + 2.0**-20
SIDE = 4
BLOCK = 256
COLS = 256
TAIL = 128
SIZES = (512, 512, 768)
ORDER = ((0, 0), (1, 0), (0, 1), (2, 0), (1, 1), (2, 1))
VMEM = 52 * 2**20


def along_y(array, step):
    perm = [(i, (i // SIDE + step) % SIDE * SIDE + i % SIDE) for i in range(SIDE * SIDE)]
    return lax.ppermute(array, "dp", perm)


def along_x(array, step):
    perm = [(i, i // SIDE * SIDE + (i % SIDE + step) % SIDE) for i in range(SIDE * SIDE)]
    return lax.ppermute(array, "dp", perm)


def swap(array, axis, bit):
    return lax.ppermute(array, axis, [(i, i ^ bit) for i in range(lax.axis_size(axis))])


def decode(codes):
    magnitude = ((codes & 7) | 8) << (((codes >> 3) & 15) - 5)
    return jnp.where(codes >= 128, -magnitude, magnitude).astype(F32)


def first_level(partial, factor):
    value = partial * factor
    magic = partial * (factor * 2.0**20)
    return jnp.clip((magic + value) - magic, -448.0, 448.0)


def next_level(one, other):
    total = one + other
    value = total * (0.5 * NUDGE)
    magic = jnp.maximum(jnp.abs(total) * 2.0**19, 1.5 * 2.0**14)
    return (magic + value) - magic


def decode_act(place, act_codes, start, size, token):
    tokens, rows = act_codes.shape
    blocks = rows // 2 // BLOCK
    first = start // BLOCK

    def kernel(place_ref, mine_ref, other_ref, *refs):
        mine_out, other_out = refs[-2:]
        mine_out[...] = decode(mine_ref[...]).T.astype(BF16)
        other_out[...] = decode(other_ref[...]).T.astype(BF16)

    extra = [] if token is None else [token]
    out = pl.BlockSpec((BLOCK, tokens), lambda i, place: (i, 0))
    return pl.pallas_call(
        kernel,
        grid_spec=pltpu.PrefetchScalarGridSpec(
            num_scalar_prefetch=1,
            grid=(size // BLOCK,),
            in_specs=[
                pl.BlockSpec((tokens, BLOCK), lambda i, p: (0, lax.rem(p[0], 2) * blocks + first + i)),
                pl.BlockSpec(
                    (tokens, BLOCK), lambda i, p: (0, (1 - lax.rem(p[0], 2)) * blocks + first + i)
                ),
            ]
            + [pl.BlockSpec(memory_space=pl.ANY)] * len(extra),
            out_specs=[out, out],
        ),
        out_shape=[jax.ShapeDtypeStruct((size, tokens), BF16)] * 2,
        compiler_params=pltpu.CompilerParams(vmem_limit_bytes=VMEM),
        cost_estimate=pl.CostEstimate(flops=0, bytes_accessed=20000 * size, transcendentals=0),
        name="decode_act",
    )(place, act_codes, act_codes, *extra)


def decode_grad(place, grad_codes, top):
    tokens, columns = grad_codes.shape
    width = SIDE * COLS

    def kernel(place_ref, code_ref, top_ref, *out_refs):
        for d in range(SIDE):
            target = lax.rem(place_ref[0] + d, SIDE)
            for b in range(2):
                owner = target if b else target + 1 - 2 * lax.rem(target, 2)
                for j in range(SIDE):
                    start = owner * width + lax.rem(place_ref[1] + j, SIDE) * COLS
                    block = decode(code_ref[:, pl.ds(pl.multiple_of(start, COLS), COLS)])
                    out_refs[b * SIDE + d][:, j * COLS : (j + 1) * COLS] = block.astype(BF16)
            filled = jnp.concatenate([top_ref[...]] * (tokens // 8), axis=0)
            out_refs[d][:, width:] = filled.astype(BF16)

    vmem = pl.BlockSpec(memory_space=pltpu.VMEM)
    out = pl.pallas_call(
        kernel,
        in_specs=[pl.BlockSpec(memory_space=pltpu.SMEM), vmem, vmem],
        out_specs=[vmem] * (2 * SIDE),
        out_shape=[jax.ShapeDtypeStruct((tokens, width + TAIL), BF16)] * SIDE
        + [jax.ShapeDtypeStruct((tokens, width), BF16)] * SIDE,
        compiler_params=pltpu.CompilerParams(vmem_limit_bytes=VMEM),
        name="decode_grad",
    )(place, grad_codes, top)
    return out[:SIDE], out[SIDE:]


def scales(gathered):
    groups, _, tokens, columns = gathered.shape

    def kernel(in_ref, scale_ref, inverse_ref):
        found = functools.reduce(
            jnp.maximum, [in_ref[t, r].astype(F32) for t in range(groups) for r in range(SIDE)]
        )
        peak = jnp.full((8, COLS), 1.0, F32) * jnp.max(found)
        scale = jnp.full_like(peak, 2.0**24)
        inverse = jnp.full_like(peak, 2.0**-24)
        for exponent in range(-16, 24):
            above = peak > 2.0**exponent
            scale = jnp.where(above, scale * 0.5, scale)
            inverse = jnp.where(above, inverse * 2.0, inverse)
        scale_ref[...] = scale * (2.0**-10 * NUDGE)
        inverse_ref[...] = inverse

    row = jax.ShapeDtypeStruct((8, COLS), F32)
    out = pl.BlockSpec((8, COLS), lambda i: (0, 0))
    return pl.pallas_call(
        kernel,
        grid=(1,),
        in_specs=[
            pl.BlockSpec((groups, SIDE, 16, TAIL), lambda i: (0, 0, 0, columns // TAIL - 1))
        ],
        out_specs=[out, out],
        out_shape=[row, row],
        name="scales",
    )(gathered)


def two_levels(factor, blocks, grads, peak, tokens_after):
    size, depth = blocks[0].shape
    groups = grads.shape[0]

    def kernel(factor_ref, own_ref, left_ref, right_ref, far_ref, grad_ref, *refs):
        old_ref, out_refs, peak_ref = refs[0], refs[-SIDE - 1 : -1], refs[-1]
        step = pl.program_id(0)

        @pl.when(step == 0)
        def _():
            peak_ref[...] = old_ref[...]

        def tile(out_ref, part):
            rows = pl.ds(part * BLOCK, BLOCK)
            levels = []
            for r, ref in enumerate((own_ref, left_ref, right_ref, far_ref)):
                grad = jnp.concatenate([grad_ref[t, r] for t in range(groups)], axis=0)
                partial = jnp.dot(ref[rows, :], grad, preferred_element_type=F32)
                size = jnp.abs(partial)
                pieces = [
                    size[8 * u : 8 * u + 8, 128 * v : 128 * v + 128]
                    for u in range(BLOCK // 8)
                    for v in range(COLS // 128)
                ]
                peak_ref[r] = jnp.maximum(peak_ref[r], functools.reduce(jnp.maximum, pieces))
                levels.append(first_level(partial, factor_ref[0:1, :]))
            level = next_level(next_level(levels[0], levels[3]), next_level(levels[1], levels[2]))
            out_ref[rows, :] = level.astype(BF16)

        for d in range(SIDE):

            @pl.when(step == d)
            def _():
                for part in range(size // BLOCK):
                    tile(out_refs[d], part)

    whole = pl.BlockSpec((size, depth), lambda j: (0, 0))
    out = pl.BlockSpec((size, COLS), lambda j: (0, 0))
    small = pl.BlockSpec((SIDE, 8, 128), lambda j: (0, 0, 0))
    *level, peak = pl.pallas_call(
        kernel,
        grid=(SIDE,),
        in_specs=[pl.BlockSpec((8, COLS), lambda j: (0, 0))]
        + [whole] * SIDE
        + [pl.BlockSpec((groups, SIDE, depth // groups, COLS), lambda j: (0, 0, 0, j)), small]
        + [pl.BlockSpec(memory_space=pl.ANY)] * len(tokens_after),
        out_specs=[out] * SIDE + [small],
        out_shape=[jax.ShapeDtypeStruct((size, COLS), BF16)] * SIDE
        + [jax.ShapeDtypeStruct((SIDE, 8, 128), F32)],
        compiler_params=pltpu.CompilerParams(vmem_limit_bytes=VMEM),
        cost_estimate=pl.CostEstimate(
            flops=16 * 10**6 * size, bytes_accessed=7000000, transcendentals=0
        ),
        name="two_levels",
    )(factor, *blocks, grads, peak, *tokens_after)
    return level, peak


def neighbour_levels(own, left, far, right):
    size = own.shape[0]

    def kernel(own_ref, left_ref, far_ref, right_ref, out_ref):
        a, b, c, d = (r[...].astype(F32) for r in (own_ref, far_ref, left_ref, right_ref))
        out_ref[...] = next_level(next_level(a, b), next_level(c, d)).astype(BF16)

    block = pl.BlockSpec((BLOCK, COLS), lambda i: (i, 0))
    return pl.pallas_call(
        kernel,
        grid=(size // BLOCK,),
        in_specs=[block] * 4,
        out_specs=block,
        out_shape=jax.ShapeDtypeStruct((size, COLS), BF16),
        compiler_params=pltpu.CompilerParams(vmem_limit_bytes=VMEM),
        cost_estimate=pl.CostEstimate(flops=0, bytes_accessed=6000000, transcendentals=0),
        name="neighbour_levels",
    )(own, left, far, right)


def last_levels(place, inverse, own, left, far, right, other, start, rows, earlier):
    size = own.shape[0]
    count = size // BLOCK
    blocks = rows // 2 // BLOCK
    first = start // BLOCK

    def kernel(place_ref, inverse_ref, own_ref, left_ref, far_ref, right_ref, other_ref, *refs):
        out_ref = refs[-1]

        @pl.when(pl.program_id(0) == 0)
        def _():
            a, b, c, d = (r[...].astype(F32) for r in (own_ref, far_ref, left_ref, right_ref))
            out_ref[...] = next_level(next_level(a, b), next_level(c, d)) * inverse_ref[0:1, :]

        @pl.when(pl.program_id(0) == 1)
        def _():
            out_ref[...] = other_ref[...].astype(F32) * inverse_ref[0:1, :]

    def out_map(s, i, place):
        side = lax.rem(place[0], 2)
        return (jnp.where(s == 0, side, 1 - side) * blocks + first + i, 0)

    mine = pl.BlockSpec((BLOCK, COLS), lambda s, i, place: (jnp.where(s == 0, i, count - 1), 0))
    extra = [] if earlier is None else [earlier]
    return pl.pallas_call(
        kernel,
        grid_spec=pltpu.PrefetchScalarGridSpec(
            num_scalar_prefetch=1,
            grid=(2, count),
            in_specs=[pl.BlockSpec((8, COLS), lambda s, i, place: (0, 0))]
            + [mine] * 4
            + [pl.BlockSpec((BLOCK, COLS), lambda s, i, place: (jnp.where(s == 1, i, 0), 0))]
            + [pl.BlockSpec(memory_space=pl.ANY)] * len(extra),
            out_specs=pl.BlockSpec((BLOCK, COLS), out_map),
        ),
        out_shape=jax.ShapeDtypeStruct((rows, COLS), F32),
        input_output_aliases={7: 0} if extra else {},
        compiler_params=pltpu.CompilerParams(vmem_limit_bytes=VMEM),
        cost_estimate=pl.CostEstimate(flops=0, bytes_accessed=6000000, transcendentals=0),
        name="last_levels",
    )(place, inverse, own, left, far, right, other, *extra)


def shards(act_codes, grad_codes, amax_history):
    position = lax.axis_index("dp")
    place = jnp.stack([position // SIDE, position % SIDE]).astype(jnp.int32)
    rows = act_codes.shape[1]
    width = SIDE * COLS

    top = jnp.full((8, 128), 1.0, F32) * jnp.max(amax_history)
    top = functools.reduce(jnp.maximum, [along_x(top, d) for d in (2, 1, 3)], top)
    grads = []
    for sent in decode_grad(place, grad_codes, top):
        from_far, from_left, from_right = (along_y(sent[d], d) for d in (2, 1, 3))
        grads.append(
            lax.all_gather(jnp.stack([sent[0], from_left, from_right, from_far]), "tensor")
        )
    factor, inverse = scales(grads[0])

    starts = [sum(SIZES[:c]) for c in range(len(SIZES))]
    acts = {}

    def send(c, token):
        mine, other = decode_act(place, act_codes, starts[c], SIZES[c], token)
        acts[c] = (mine, along_y(other, 1), along_y(other, 3), along_y(mine, 2))

    peak = jnp.zeros((SIDE, 8, 128), F32)
    levels, sides = {}, {}
    weight_grad = None
    for c in range(len(SIZES)):
        send(c, None)
    waits = []
    for c, b in ORDER:
        after = levels[waits[-2]][1:] if len(waits) > 1 else ()
        level, peak = two_levels(factor, acts[c], grads[b], peak, after)
        levels[c, b] = (level[0], along_x(level[1], 1), along_x(level[2], 2), along_x(level[3], 3))
        waits.append((c, b))
        if b == 0:
            sides[c] = swap(neighbour_levels(*levels[c, b]), "dp", SIDE)
        else:
            weight_grad = last_levels(
                place, inverse, *levels[c, b], sides[c], starts[c], rows, weight_grad
            )

    others = (along_y(peak[1], 3), along_y(peak[2], 1), along_y(peak[3], 2))
    current = jnp.max(functools.reduce(jnp.maximum, others, peak[0])) * 2.0**-10
    new_history = jnp.concatenate([current.reshape(1, 1), amax_history[:, :-1]], axis=1)
    return weight_grad, new_history


def solution(mesh):
    return jax.shard_map(
        shards,
        mesh=mesh,
        in_specs=(P("dp", "tensor"), P(("dp", "tensor"), None), P(("dp", "tensor"), None)),
        out_specs=(P("tensor", "dp"), P(("dp", "tensor"), None)),
        check_vma=False,
    )
```

```python
import functools

import jax
import jax.numpy as jnp
from jax import lax
from jax.experimental import pallas as pl
from jax.experimental.pallas import tpu as pltpu
from jax.sharding import PartitionSpec as P

F32 = jnp.float32
BF16 = jnp.bfloat16
NUDGE = 1.0 + 2.0**-20
SIDE = 4
BLOCK = 256
COLS = 256
TAIL = 128
SIZES = (512, 512, 768)
ORDER = (
    (0, 0, (), ()),
    (1, 0, (), ()),
    (0, 1, (), ()),
    (1, 1, (2,), ()),
    (2, 0, (), (0,)),
    (2, 1, (), (1,)),
)
VMEM = 52 * 2**20


def along_y(array, step):
    perm = [(i, (i // SIDE + step) % SIDE * SIDE + i % SIDE) for i in range(SIDE * SIDE)]
    return lax.ppermute(array, "dp", perm)


def along_x(array, step):
    perm = [(i, i // SIDE * SIDE + (i % SIDE + step) % SIDE) for i in range(SIDE * SIDE)]
    return lax.ppermute(array, "dp", perm)


def swap(array, axis, bit):
    return lax.ppermute(array, axis, [(i, i ^ bit) for i in range(lax.axis_size(axis))])


def decode(codes):
    magnitude = ((codes & 7) | 8) << (((codes >> 3) & 15) - 5)
    return jnp.where(codes >= 128, -magnitude, magnitude).astype(F32)


def first_level(partial, factor):
    value = partial * factor
    magic = partial * (factor * 2.0**20)
    return jnp.clip((magic + value) - magic, -448.0, 448.0)


def next_level(one, other):
    total = one + other
    value = total * (0.5 * NUDGE)
    magic = jnp.maximum(jnp.abs(total) * 2.0**19, 1.5 * 2.0**14)
    return (magic + value) - magic


def decode_act(place, act_codes, start, size, extra):
    tokens, rows = act_codes.shape
    blocks = rows // 2 // BLOCK
    first = start // BLOCK

    def kernel(place_ref, mine_ref, other_ref, *refs):
        mine_out, other_out = refs[-2:]
        mine_out[...] = decode(mine_ref[...]).T.astype(BF16)
        other_out[...] = decode(other_ref[...]).T.astype(BF16)

    out = pl.BlockSpec((BLOCK, tokens), lambda i, place: (i, 0))
    return pl.pallas_call(
        kernel,
        grid_spec=pltpu.PrefetchScalarGridSpec(
            num_scalar_prefetch=1,
            grid=(size // BLOCK,),
            in_specs=[
                pl.BlockSpec((tokens, BLOCK), lambda i, p: (0, lax.rem(p[0], 2) * blocks + first + i)),
                pl.BlockSpec(
                    (tokens, BLOCK), lambda i, p: (0, (1 - lax.rem(p[0], 2)) * blocks + first + i)
                ),
            ]
            + [pl.BlockSpec(memory_space=pl.ANY)] * len(extra),
            out_specs=[out, out],
        ),
        out_shape=[jax.ShapeDtypeStruct((size, tokens), BF16)] * 2,
        compiler_params=pltpu.CompilerParams(vmem_limit_bytes=VMEM),
        cost_estimate=pl.CostEstimate(flops=0, bytes_accessed=20000 * size, transcendentals=0),
        name="decode_act",
    )(place, act_codes, act_codes, *extra)


def decode_grad(place, grad_codes, top, extra):
    tokens, columns = grad_codes.shape
    width = SIDE * COLS

    def kernel(place_ref, code_ref, top_ref, *refs):
        out_refs = refs[len(extra) :]
        for d in range(SIDE):
            target = lax.rem(place_ref[0] + d, SIDE)
            for b in range(2):
                owner = target if b else target + 1 - 2 * lax.rem(target, 2)
                for j in range(SIDE):
                    start = owner * width + lax.rem(place_ref[1] + j, SIDE) * COLS
                    block = decode(code_ref[:, pl.ds(pl.multiple_of(start, COLS), COLS)])
                    out_refs[b * SIDE + d][:, j * COLS : (j + 1) * COLS] = block.astype(BF16)
            filled = jnp.concatenate([top_ref[...]] * (tokens // 8), axis=0)
            out_refs[d][:, width:] = filled.astype(BF16)

    vmem = pl.BlockSpec(memory_space=pltpu.VMEM)
    out = pl.pallas_call(
        kernel,
        in_specs=[pl.BlockSpec(memory_space=pltpu.SMEM), vmem, vmem]
        + [pl.BlockSpec(memory_space=pl.ANY)] * len(extra),
        out_specs=[vmem] * (2 * SIDE),
        out_shape=[jax.ShapeDtypeStruct((tokens, width + TAIL), BF16)] * SIDE
        + [jax.ShapeDtypeStruct((tokens, width), BF16)] * SIDE,
        compiler_params=pltpu.CompilerParams(vmem_limit_bytes=VMEM),
        name="decode_grad",
    )(place, grad_codes, top, *extra)
    return out[:SIDE], out[SIDE:]


def pack(parts, extra):
    def kernel(*refs):
        for r in range(SIDE):
            refs[-1][r] = refs[r][...]

    vmem = pl.BlockSpec(memory_space=pltpu.VMEM)
    return pl.pallas_call(
        kernel,
        in_specs=[vmem] * SIDE + [pl.BlockSpec(memory_space=pl.ANY)] * len(extra),
        out_specs=vmem,
        out_shape=jax.ShapeDtypeStruct((SIDE,) + parts[0].shape, BF16),
        name="pack",
    )(*parts, *extra)


def unjoin(own, joined, size, extra):
    tokens, width = own.shape
    rows, depth = joined[0].shape

    def kernel(own_ref, *refs):
        out_ref = refs[-1]
        out_ref[0] = own_ref[...]
        for r in range(1, SIDE):
            for v in range(width // depth):
                piece = refs[r - 1][v * tokens : (v + 1) * tokens, :]
                out_ref[r, :, v * depth : (v + 1) * depth] = piece

    last = pl.BlockSpec((rows - size, depth), lambda i: (size // (rows - size), 0))
    return pl.pallas_call(
        kernel,
        grid=(1,),
        in_specs=[pl.BlockSpec((tokens, width), lambda i: (0, 0))]
        + [last] * (SIDE - 1)
        + [pl.BlockSpec(memory_space=pl.ANY)] * len(extra),
        out_specs=pl.BlockSpec((SIDE, tokens, width), lambda i: (0, 0, 0)),
        out_shape=jax.ShapeDtypeStruct((SIDE, tokens, width), BF16),
        name="unjoin",
    )(own, *joined, *extra)


def join(acts, grads):
    size, depth = acts[0].shape
    tokens, width = grads[0].shape
    pieces = width // depth

    def kernel(*refs):
        for k in range(len(acts)):
            act_ref, grad_ref, out_ref = refs[k], refs[len(acts) + k], refs[2 * len(acts) + k]
            out_ref[:size, :] = act_ref[...]
            for v in range(pieces):
                at = size + v * tokens
                out_ref[at : at + tokens, :] = grad_ref[:, v * depth : (v + 1) * depth]

    vmem = pl.BlockSpec(memory_space=pltpu.VMEM)
    return pl.pallas_call(
        kernel,
        in_specs=[vmem] * (2 * len(acts)),
        out_specs=[vmem] * len(acts),
        out_shape=[jax.ShapeDtypeStruct((size + pieces * tokens, depth), BF16)] * len(acts),
        compiler_params=pltpu.CompilerParams(vmem_limit_bytes=VMEM),
        name="join",
    )(*acts, *grads)


def scales(gathered):
    groups, _, tokens, columns = gathered.shape

    def kernel(in_ref, scale_ref, inverse_ref):
        found = functools.reduce(
            jnp.maximum, [in_ref[t, r].astype(F32) for t in range(groups) for r in range(SIDE)]
        )
        peak = jnp.full((8, COLS), 1.0, F32) * jnp.max(found)
        scale = jnp.full_like(peak, 2.0**24)
        inverse = jnp.full_like(peak, 2.0**-24)
        for exponent in range(-16, 24):
            above = peak > 2.0**exponent
            scale = jnp.where(above, scale * 0.5, scale)
            inverse = jnp.where(above, inverse * 2.0, inverse)
        scale_ref[...] = scale * (2.0**-10 * NUDGE)
        inverse_ref[...] = inverse

    row = jax.ShapeDtypeStruct((8, COLS), F32)
    out = pl.BlockSpec((8, COLS), lambda i: (0, 0))
    return pl.pallas_call(
        kernel,
        grid=(1,),
        in_specs=[
            pl.BlockSpec((groups, SIDE, 16, TAIL), lambda i: (0, 0, 0, columns // TAIL - 1))
        ],
        out_specs=[out, out],
        out_shape=[row, row],
        name="scales",
    )(gathered)


def two_levels(factor, blocks, size, grads, peak, tokens_after):
    depth = blocks[0].shape[1]
    groups = grads.shape[0]

    def kernel(factor_ref, own_ref, left_ref, right_ref, far_ref, grad_ref, *refs):
        old_ref, out_refs, peak_ref = refs[0], refs[-SIDE - 1 : -1], refs[-1]
        step = pl.program_id(0)

        @pl.when(step == 0)
        def _():
            peak_ref[...] = old_ref[...]

        def tile(out_ref, part):
            rows = pl.ds(part * BLOCK, BLOCK)
            levels = []
            for r, ref in enumerate((own_ref, left_ref, right_ref, far_ref)):
                grad = jnp.concatenate([grad_ref[t, r] for t in range(groups)], axis=0)
                partial = jnp.dot(ref[rows, :], grad, preferred_element_type=F32)
                absolute = jnp.abs(partial)
                pieces = [
                    absolute[8 * u : 8 * u + 8, 128 * v : 128 * v + 128]
                    for u in range(BLOCK // 8)
                    for v in range(COLS // 128)
                ]
                peak_ref[r] = jnp.maximum(peak_ref[r], functools.reduce(jnp.maximum, pieces))
                levels.append(first_level(partial, factor_ref[0:1, :]))
            level = next_level(next_level(levels[0], levels[3]), next_level(levels[1], levels[2]))
            out_ref[rows, :] = level.astype(BF16)

        for d in range(SIDE):

            @pl.when(step == d)
            def _():
                for part in range(size // BLOCK):
                    tile(out_refs[d], part)

    whole = pl.BlockSpec((size, depth), lambda j: (0, 0))
    out = pl.BlockSpec((size, COLS), lambda j: (0, 0))
    small = pl.BlockSpec((SIDE, 8, 128), lambda j: (0, 0, 0))
    *level, peak = pl.pallas_call(
        kernel,
        grid=(SIDE,),
        in_specs=[pl.BlockSpec((8, COLS), lambda j: (0, 0))]
        + [whole] * SIDE
        + [pl.BlockSpec((groups, SIDE, depth // groups, COLS), lambda j: (0, 0, 0, j)), small]
        + [pl.BlockSpec(memory_space=pl.ANY)] * len(tokens_after),
        out_specs=[out] * SIDE + [small],
        out_shape=[jax.ShapeDtypeStruct((size, COLS), BF16)] * SIDE
        + [jax.ShapeDtypeStruct((SIDE, 8, 128), F32)],
        compiler_params=pltpu.CompilerParams(vmem_limit_bytes=VMEM),
        cost_estimate=pl.CostEstimate(
            flops=16 * 10**6 * size, bytes_accessed=7000000, transcendentals=0
        ),
        name="two_levels",
    )(factor, *blocks, grads, peak, *tokens_after)
    return level, peak


def neighbour_levels(own, left, far, right):
    size = own.shape[0]

    def kernel(own_ref, left_ref, far_ref, right_ref, out_ref):
        a, b, c, d = (r[...].astype(F32) for r in (own_ref, far_ref, left_ref, right_ref))
        out_ref[...] = next_level(next_level(a, b), next_level(c, d)).astype(BF16)

    block = pl.BlockSpec((BLOCK, COLS), lambda i: (i, 0))
    return pl.pallas_call(
        kernel,
        grid=(size // BLOCK,),
        in_specs=[block] * 4,
        out_specs=block,
        out_shape=jax.ShapeDtypeStruct((size, COLS), BF16),
        compiler_params=pltpu.CompilerParams(vmem_limit_bytes=VMEM),
        cost_estimate=pl.CostEstimate(flops=0, bytes_accessed=6000000, transcendentals=0),
        name="neighbour_levels",
    )(own, left, far, right)


def last_levels(place, inverse, own, left, far, right, other, start, rows, earlier):
    size = own.shape[0]
    count = size // BLOCK
    blocks = rows // 2 // BLOCK
    first = start // BLOCK

    def kernel(place_ref, inverse_ref, own_ref, left_ref, far_ref, right_ref, other_ref, *refs):
        out_ref = refs[-1]

        @pl.when(pl.program_id(0) == 0)
        def _():
            a, b, c, d = (r[...].astype(F32) for r in (own_ref, far_ref, left_ref, right_ref))
            out_ref[...] = next_level(next_level(a, b), next_level(c, d)) * inverse_ref[0:1, :]

        @pl.when(pl.program_id(0) == 1)
        def _():
            out_ref[...] = other_ref[...].astype(F32) * inverse_ref[0:1, :]

    def out_map(s, i, place):
        side = lax.rem(place[0], 2)
        return (jnp.where(s == 0, side, 1 - side) * blocks + first + i, 0)

    mine = pl.BlockSpec((BLOCK, COLS), lambda s, i, place: (jnp.where(s == 0, i, count - 1), 0))
    extra = [] if earlier is None else [earlier]
    return pl.pallas_call(
        kernel,
        grid_spec=pltpu.PrefetchScalarGridSpec(
            num_scalar_prefetch=1,
            grid=(2, count),
            in_specs=[pl.BlockSpec((8, COLS), lambda s, i, place: (0, 0))]
            + [mine] * 4
            + [pl.BlockSpec((BLOCK, COLS), lambda s, i, place: (jnp.where(s == 1, i, 0), 0))]
            + [pl.BlockSpec(memory_space=pl.ANY)] * len(extra),
            out_specs=pl.BlockSpec((BLOCK, COLS), out_map),
        ),
        out_shape=jax.ShapeDtypeStruct((rows, COLS), F32),
        input_output_aliases={7: 0} if extra else {},
        compiler_params=pltpu.CompilerParams(vmem_limit_bytes=VMEM),
        cost_estimate=pl.CostEstimate(flops=0, bytes_accessed=6000000, transcendentals=0),
        name="last_levels",
    )(place, inverse, own, left, far, right, other, *extra)


def shards(act_codes, grad_codes, amax_history):
    position = lax.axis_index("dp")
    place = jnp.stack([position // SIDE, position % SIDE]).astype(jnp.int32)
    rows = act_codes.shape[1]
    top = jnp.full((8, 128), 1.0, F32) * jnp.max(amax_history)
    top = functools.reduce(jnp.maximum, [along_x(top, d) for d in (2, 1, 3)], top)
    starts = [sum(SIZES[:c]) for c in range(len(SIZES))]
    codes = [decode_act(place, act_codes, starts[c], SIZES[c], []) for c in range(len(SIZES))]
    sent = decode_grad(place, grad_codes, top, [codes[0][0]])

    def arrive(c):
        mine, other = codes[c]
        return (mine, along_y(other, 1), along_y(other, 3), along_y(mine, 2))

    mine, other = codes[0]
    joined = join([other, other, mine], [sent[1][d] for d in (1, 3, 2)])
    parts = [sent[0][0]] + [along_y(sent[0][d], d) for d in (1, 3, 2)]
    grads = [lax.all_gather(pack(parts, joined[:1]), "tensor")]
    factor, inverse = scales(grads[0])
    acts = [(mine,) + tuple(along_y(array, d) for array, d in zip(joined, (1, 3, 2)))]
    parts = unjoin(sent[1][0], acts[0][1:], SIZES[0], [mine for mine, _ in codes])
    grads.append(lax.all_gather(parts, "tensor"))
    acts += [arrive(c) for c in range(1, len(SIZES))]

    peak = jnp.zeros((SIDE, 8, 128), F32)
    levels, sides, done = {}, {}, []
    weight_grad = None
    for c, b, ahead, passed in ORDER:
        extra = list(levels[done[-2]][1:]) if len(done) > 1 else []
        extra += [acts[k][1] for k in ahead] + [sides[k] for k in passed]
        level, peak = two_levels(factor, acts[c], SIZES[c], grads[b], peak, extra)
        levels[c, b] = (level[0], along_x(level[1], 1), along_x(level[2], 2), along_x(level[3], 3))
        done.append((c, b))
        if b == 0:
            sides[c] = swap(neighbour_levels(*levels[c, b]), "dp", SIDE)
        else:
            weight_grad = last_levels(
                place, inverse, *levels[c, b], sides[c], starts[c], rows, weight_grad
            )

    others = (along_y(peak[1], 3), along_y(peak[2], 1), along_y(peak[3], 2))
    current = jnp.max(functools.reduce(jnp.maximum, others, peak[0])) * 2.0**-10
    new_history = jnp.concatenate([current.reshape(1, 1), amax_history[:, :-1]], axis=1)
    return weight_grad, new_history


def solution(mesh):
    return jax.shard_map(
        shards,
        mesh=mesh,
        in_specs=(P("dp", "tensor"), P(("dp", "tensor"), None), P(("dp", "tensor"), None)),
        out_specs=(P("tensor", "dp"), P(("dp", "tensor"), None)),
        check_vma=False,
    )
```

```python
import functools

import jax
import jax.numpy as jnp
from jax import lax
from jax.experimental import pallas as pl
from jax.experimental.pallas import tpu as pltpu
from jax.sharding import PartitionSpec as P

F32 = jnp.float32
BF16 = jnp.bfloat16
NUDGE = 1.0 + 2.0**-20
SIDE = 4
BLOCK = 256
COLS = 256
TAIL = 128
SIZES = (768, 512, 512)
ORDER = (
    (0, 0, (), ()),
    (1, 0, (), ()),
    (0, 1, (), ()),
    (1, 1, (2,), ()),
    (2, 0, (), (0,)),
    (2, 1, (), (1,)),
)
VMEM = 52 * 2**20


def along_y(array, step):
    perm = [(i, (i // SIDE + step) % SIDE * SIDE + i % SIDE) for i in range(SIDE * SIDE)]
    return lax.ppermute(array, "dp", perm)


def along_x(array, step):
    perm = [(i, i // SIDE * SIDE + (i % SIDE + step) % SIDE) for i in range(SIDE * SIDE)]
    return lax.ppermute(array, "dp", perm)


def swap(array, axis, bit):
    return lax.ppermute(array, axis, [(i, i ^ bit) for i in range(lax.axis_size(axis))])


def decode(codes):
    magnitude = ((codes & 7) | 8) << (((codes >> 3) & 15) - 5)
    return jnp.where(codes >= 128, -magnitude, magnitude).astype(F32)


def first_level(partial, factor):
    value = partial * factor
    magic = partial * (factor * 2.0**20)
    return jnp.clip((magic + value) - magic, -448.0, 448.0)


def next_level(one, other):
    total = one + other
    value = total * (0.5 * NUDGE)
    magic = jnp.maximum(jnp.abs(total) * 2.0**19, 1.5 * 2.0**14)
    return (magic + value) - magic


def decode_act(place, act_codes, start, size, extra):
    tokens, rows = act_codes.shape
    blocks = rows // 2 // BLOCK
    first = start // BLOCK

    def kernel(place_ref, mine_ref, other_ref, *refs):
        mine_out, other_out = refs[-2:]
        mine_out[...] = decode(mine_ref[...]).T.astype(BF16)
        other_out[...] = decode(other_ref[...]).T.astype(BF16)

    out = pl.BlockSpec((BLOCK, tokens), lambda i, place: (i, 0))
    return pl.pallas_call(
        kernel,
        grid_spec=pltpu.PrefetchScalarGridSpec(
            num_scalar_prefetch=1,
            grid=(size // BLOCK,),
            in_specs=[
                pl.BlockSpec((tokens, BLOCK), lambda i, p: (0, lax.rem(p[0], 2) * blocks + first + i)),
                pl.BlockSpec(
                    (tokens, BLOCK), lambda i, p: (0, (1 - lax.rem(p[0], 2)) * blocks + first + i)
                ),
            ]
            + [pl.BlockSpec(memory_space=pl.ANY)] * len(extra),
            out_specs=[out, out],
        ),
        out_shape=[jax.ShapeDtypeStruct((size, tokens), BF16)] * 2,
        compiler_params=pltpu.CompilerParams(vmem_limit_bytes=VMEM),
        cost_estimate=pl.CostEstimate(flops=0, bytes_accessed=20000 * size, transcendentals=0),
        name="decode_act",
    )(place, act_codes, act_codes, *extra)


def decode_grad(place, grad_codes, top, extra):
    tokens, columns = grad_codes.shape
    width = SIDE * COLS

    def kernel(place_ref, code_ref, top_ref, *refs):
        out_refs = refs[len(extra) :]
        for d in range(SIDE):
            target = lax.rem(place_ref[0] + d, SIDE)
            for b in range(2):
                owner = target if b else target + 1 - 2 * lax.rem(target, 2)
                for j in range(SIDE):
                    start = owner * width + lax.rem(place_ref[1] + j, SIDE) * COLS
                    block = decode(code_ref[:, pl.ds(pl.multiple_of(start, COLS), COLS)])
                    out_refs[b * SIDE + d][:, j * COLS : (j + 1) * COLS] = block.astype(BF16)
            filled = jnp.concatenate([top_ref[...]] * (tokens // 8), axis=0)
            out_refs[d][:, width:] = filled.astype(BF16)

    vmem = pl.BlockSpec(memory_space=pltpu.VMEM)
    out = pl.pallas_call(
        kernel,
        in_specs=[pl.BlockSpec(memory_space=pltpu.SMEM), vmem, vmem]
        + [pl.BlockSpec(memory_space=pl.ANY)] * len(extra),
        out_specs=[vmem] * (2 * SIDE),
        out_shape=[jax.ShapeDtypeStruct((tokens, width + TAIL), BF16)] * SIDE
        + [jax.ShapeDtypeStruct((tokens, width), BF16)] * SIDE,
        compiler_params=pltpu.CompilerParams(vmem_limit_bytes=VMEM),
        name="decode_grad",
    )(place, grad_codes, top, *extra)
    return out[:SIDE], out[SIDE:]


def pack(parts, extra):
    def kernel(*refs):
        for r in range(SIDE):
            refs[-1][r] = refs[r][...]

    vmem = pl.BlockSpec(memory_space=pltpu.VMEM)
    return pl.pallas_call(
        kernel,
        in_specs=[vmem] * SIDE + [pl.BlockSpec(memory_space=pl.ANY)] * len(extra),
        out_specs=vmem,
        out_shape=jax.ShapeDtypeStruct((SIDE,) + parts[0].shape, BF16),
        name="pack",
    )(*parts, *extra)


def unjoin(own, joined, size, extra):
    tokens, width = own.shape
    rows, depth = joined[0].shape

    def kernel(own_ref, *refs):
        out_ref = refs[-1]
        out_ref[0] = own_ref[...]
        for r in range(1, SIDE):
            for v in range(width // depth):
                piece = refs[r - 1][v * tokens : (v + 1) * tokens, :]
                out_ref[r, :, v * depth : (v + 1) * depth] = piece

    last = pl.BlockSpec((rows - size, depth), lambda i: (size // (rows - size), 0))
    return pl.pallas_call(
        kernel,
        grid=(1,),
        in_specs=[pl.BlockSpec((tokens, width), lambda i: (0, 0))]
        + [last] * (SIDE - 1)
        + [pl.BlockSpec(memory_space=pl.ANY)] * len(extra),
        out_specs=pl.BlockSpec((SIDE, tokens, width), lambda i: (0, 0, 0)),
        out_shape=jax.ShapeDtypeStruct((SIDE, tokens, width), BF16),
        name="unjoin",
    )(own, *joined, *extra)


def join(acts, grads):
    size, depth = acts[0].shape
    tokens, width = grads[0].shape
    pieces = width // depth

    def kernel(*refs):
        for k in range(len(acts)):
            act_ref, grad_ref, out_ref = refs[k], refs[len(acts) + k], refs[2 * len(acts) + k]
            out_ref[:size, :] = act_ref[...]
            for v in range(pieces):
                at = size + v * tokens
                out_ref[at : at + tokens, :] = grad_ref[:, v * depth : (v + 1) * depth]

    vmem = pl.BlockSpec(memory_space=pltpu.VMEM)
    return pl.pallas_call(
        kernel,
        in_specs=[vmem] * (2 * len(acts)),
        out_specs=[vmem] * len(acts),
        out_shape=[jax.ShapeDtypeStruct((size + pieces * tokens, depth), BF16)] * len(acts),
        compiler_params=pltpu.CompilerParams(vmem_limit_bytes=VMEM),
        name="join",
    )(*acts, *grads)


def scales(gathered):
    groups, _, tokens, columns = gathered.shape

    def kernel(in_ref, scale_ref, inverse_ref):
        found = functools.reduce(
            jnp.maximum, [in_ref[t, r].astype(F32) for t in range(groups) for r in range(SIDE)]
        )
        peak = jnp.full((8, COLS), 1.0, F32) * jnp.max(found)
        scale = jnp.full_like(peak, 2.0**24)
        inverse = jnp.full_like(peak, 2.0**-24)
        for exponent in range(-16, 24):
            above = peak > 2.0**exponent
            scale = jnp.where(above, scale * 0.5, scale)
            inverse = jnp.where(above, inverse * 2.0, inverse)
        scale_ref[...] = scale * (2.0**-10 * NUDGE)
        inverse_ref[...] = inverse

    row = jax.ShapeDtypeStruct((8, COLS), F32)
    out = pl.BlockSpec((8, COLS), lambda i: (0, 0))
    return pl.pallas_call(
        kernel,
        grid=(1,),
        in_specs=[
            pl.BlockSpec((groups, SIDE, 16, TAIL), lambda i: (0, 0, 0, columns // TAIL - 1))
        ],
        out_specs=[out, out],
        out_shape=[row, row],
        name="scales",
    )(gathered)


def two_levels(factor, blocks, size, grads, peak, tokens_after):
    depth = blocks[0].shape[1]
    groups = grads.shape[0]

    def kernel(factor_ref, own_ref, left_ref, right_ref, far_ref, grad_ref, *refs):
        old_ref, out_refs, peak_ref = refs[0], refs[-SIDE - 1 : -1], refs[-1]
        step = pl.program_id(0)

        @pl.when(step == 0)
        def _():
            peak_ref[...] = old_ref[...]

        def tile(out_ref, part):
            rows = pl.ds(part * BLOCK, BLOCK)
            levels = []
            for r, ref in enumerate((own_ref, left_ref, right_ref, far_ref)):
                grad = jnp.concatenate([grad_ref[t, r] for t in range(groups)], axis=0)
                partial = jnp.dot(ref[rows, :], grad, preferred_element_type=F32)
                absolute = jnp.abs(partial)
                pieces = [
                    absolute[8 * u : 8 * u + 8, 128 * v : 128 * v + 128]
                    for u in range(BLOCK // 8)
                    for v in range(COLS // 128)
                ]
                peak_ref[r] = jnp.maximum(peak_ref[r], functools.reduce(jnp.maximum, pieces))
                levels.append(first_level(partial, factor_ref[0:1, :]))
            level = next_level(next_level(levels[0], levels[3]), next_level(levels[1], levels[2]))
            out_ref[rows, :] = level.astype(BF16)

        for d in range(SIDE):

            @pl.when(step == d)
            def _():
                for part in range(size // BLOCK):
                    tile(out_refs[d], part)

    whole = pl.BlockSpec((size, depth), lambda j: (0, 0))
    out = pl.BlockSpec((size, COLS), lambda j: (0, 0))
    small = pl.BlockSpec((SIDE, 8, 128), lambda j: (0, 0, 0))
    *level, peak = pl.pallas_call(
        kernel,
        grid=(SIDE,),
        in_specs=[pl.BlockSpec((8, COLS), lambda j: (0, 0))]
        + [whole] * SIDE
        + [pl.BlockSpec((groups, SIDE, depth // groups, COLS), lambda j: (0, 0, 0, j)), small]
        + [pl.BlockSpec(memory_space=pl.ANY)] * len(tokens_after),
        out_specs=[out] * SIDE + [small],
        out_shape=[jax.ShapeDtypeStruct((size, COLS), BF16)] * SIDE
        + [jax.ShapeDtypeStruct((SIDE, 8, 128), F32)],
        compiler_params=pltpu.CompilerParams(vmem_limit_bytes=VMEM),
        cost_estimate=pl.CostEstimate(
            flops=16 * 10**6 * size, bytes_accessed=7000000, transcendentals=0
        ),
        name="two_levels",
    )(factor, *blocks, grads, peak, *tokens_after)
    return level, peak


def neighbour_levels(own, left, far, right):
    size = own.shape[0]

    def kernel(own_ref, left_ref, far_ref, right_ref, out_ref):
        a, b, c, d = (r[...].astype(F32) for r in (own_ref, far_ref, left_ref, right_ref))
        out_ref[...] = next_level(next_level(a, b), next_level(c, d)).astype(BF16)

    block = pl.BlockSpec((BLOCK, COLS), lambda i: (i, 0))
    return pl.pallas_call(
        kernel,
        grid=(size // BLOCK,),
        in_specs=[block] * 4,
        out_specs=block,
        out_shape=jax.ShapeDtypeStruct((size, COLS), BF16),
        compiler_params=pltpu.CompilerParams(vmem_limit_bytes=VMEM),
        cost_estimate=pl.CostEstimate(flops=0, bytes_accessed=6000000, transcendentals=0),
        name="neighbour_levels",
    )(own, left, far, right)


def last_levels(place, inverse, own, left, far, right, other, start, rows, earlier):
    size = own.shape[0]
    count = size // BLOCK
    blocks = rows // 2 // BLOCK
    first = start // BLOCK

    def kernel(place_ref, inverse_ref, own_ref, left_ref, far_ref, right_ref, other_ref, *refs):
        out_ref = refs[-1]

        @pl.when(pl.program_id(0) == 0)
        def _():
            a, b, c, d = (r[...].astype(F32) for r in (own_ref, far_ref, left_ref, right_ref))
            out_ref[...] = next_level(next_level(a, b), next_level(c, d)) * inverse_ref[0:1, :]

        @pl.when(pl.program_id(0) == 1)
        def _():
            out_ref[...] = other_ref[...].astype(F32) * inverse_ref[0:1, :]

    def out_map(s, i, place):
        side = lax.rem(place[0], 2)
        return (jnp.where(s == 0, side, 1 - side) * blocks + first + i, 0)

    mine = pl.BlockSpec((BLOCK, COLS), lambda s, i, place: (jnp.where(s == 0, i, count - 1), 0))
    extra = [] if earlier is None else [earlier]
    return pl.pallas_call(
        kernel,
        grid_spec=pltpu.PrefetchScalarGridSpec(
            num_scalar_prefetch=1,
            grid=(2, count),
            in_specs=[pl.BlockSpec((8, COLS), lambda s, i, place: (0, 0))]
            + [mine] * 4
            + [pl.BlockSpec((BLOCK, COLS), lambda s, i, place: (jnp.where(s == 1, i, 0), 0))]
            + [pl.BlockSpec(memory_space=pl.ANY)] * len(extra),
            out_specs=pl.BlockSpec((BLOCK, COLS), out_map),
        ),
        out_shape=jax.ShapeDtypeStruct((rows, COLS), F32),
        input_output_aliases={7: 0} if extra else {},
        compiler_params=pltpu.CompilerParams(vmem_limit_bytes=VMEM),
        cost_estimate=pl.CostEstimate(flops=0, bytes_accessed=6000000, transcendentals=0),
        name="last_levels",
    )(place, inverse, own, left, far, right, other, *extra)


def shards(act_codes, grad_codes, amax_history):
    position = lax.axis_index("dp")
    place = jnp.stack([position // SIDE, position % SIDE]).astype(jnp.int32)
    rows = act_codes.shape[1]
    top = jnp.full((8, 128), 1.0, F32) * jnp.max(amax_history)
    top = functools.reduce(jnp.maximum, [along_x(top, d) for d in (2, 1, 3)], top)
    starts = [sum(SIZES[:c]) for c in range(len(SIZES))]
    codes = [decode_act(place, act_codes, starts[c], SIZES[c], []) for c in range(len(SIZES))]
    sent = decode_grad(place, grad_codes, top, [codes[0][0]])

    def arrive(c):
        mine, other = codes[c]
        return (mine, along_y(other, 1), along_y(other, 3), along_y(mine, 2))

    mine, other = codes[0]
    joined = join([other, other, mine], [sent[1][d] for d in (1, 3, 2)])
    parts = [sent[0][0]] + [along_y(sent[0][d], d) for d in (1, 3, 2)]
    grads = [lax.all_gather(pack(parts, joined[:1]), "tensor")]
    factor, inverse = scales(grads[0])
    acts = [(mine,) + tuple(along_y(array, d) for array, d in zip(joined, (1, 3, 2)))]
    parts = unjoin(sent[1][0], acts[0][1:], SIZES[0], [mine for mine, _ in codes])
    grads.append(lax.all_gather(parts, "tensor"))
    acts += [arrive(c) for c in range(1, len(SIZES))]

    peak = jnp.zeros((SIDE, 8, 128), F32)
    levels, sides, done = {}, {}, []
    weight_grad = None
    for c, b, ahead, passed in ORDER:
        extra = list(levels[done[-2]][1:]) if len(done) > 1 else []
        extra += [acts[k][1] for k in ahead] + [sides[k] for k in passed]
        level, peak = two_levels(factor, acts[c], SIZES[c], grads[b], peak, extra)
        levels[c, b] = (level[0], along_x(level[1], 1), along_x(level[2], 2), along_x(level[3], 3))
        done.append((c, b))
        if b == 0:
            sides[c] = swap(neighbour_levels(*levels[c, b]), "dp", SIDE)
        else:
            weight_grad = last_levels(
                place, inverse, *levels[c, b], sides[c], starts[c], rows, weight_grad
            )

    others = (along_y(peak[1], 3), along_y(peak[2], 1), along_y(peak[3], 2))
    current = jnp.max(functools.reduce(jnp.maximum, others, peak[0])) * 2.0**-10
    new_history = jnp.concatenate([current.reshape(1, 1), amax_history[:, :-1]], axis=1)
    return weight_grad, new_history


def solution(mesh):
    return jax.shard_map(
        shards,
        mesh=mesh,
        in_specs=(P("dp", "tensor"), P(("dp", "tensor"), None), P(("dp", "tensor"), None)),
        out_specs=(P("tensor", "dp"), P(("dp", "tensor"), None)),
        check_vma=False,
    )
```

```python
import functools

import jax
import jax.numpy as jnp
from jax import lax
from jax.experimental import pallas as pl
from jax.experimental.pallas import tpu as pltpu
from jax.sharding import PartitionSpec as P

F32 = jnp.float32
BF16 = jnp.bfloat16
NUDGE = 1.0 + 2.0**-20
SIDE = 4
BLOCK = 256
COLS = 256
TAIL = 128
SIZES = (512, 512, 768)
ORDER = (
    (0, 0, (), ()),
    (1, 0, (), ()),
    (0, 1, (), ()),
    (1, 1, (2,), ()),
    (2, 0, (), (0,)),
    (2, 1, (), (1,)),
)
VMEM = 52 * 2**20


def along_y(array, step):
    perm = [(i, (i // SIDE + step) % SIDE * SIDE + i % SIDE) for i in range(SIDE * SIDE)]
    return lax.ppermute(array, "dp", perm)


def along_x(array, step):
    perm = [(i, i // SIDE * SIDE + (i % SIDE + step) % SIDE) for i in range(SIDE * SIDE)]
    return lax.ppermute(array, "dp", perm)


def swap(array, axis, bit):
    return lax.ppermute(array, axis, [(i, i ^ bit) for i in range(lax.axis_size(axis))])


def decode(codes):
    magnitude = ((codes & 7) | 8) << (((codes >> 3) & 15) - 5)
    return jnp.where(codes >= 128, -magnitude, magnitude).astype(F32)


def to_grid(value):
    return value.astype(jnp.float8_e4m3fn).astype(F32)


def first_level(partial, factor):
    return to_grid(jnp.clip(partial * factor, -448.0, 448.0))


def next_level(one, other):
    return to_grid((one + other) * (0.5 * NUDGE))


def decode_act(place, act_codes, start, size, extra):
    tokens, rows = act_codes.shape
    blocks = rows // 2 // BLOCK
    first = start // BLOCK

    def kernel(place_ref, mine_ref, other_ref, *refs):
        mine_out, other_out = refs[-2:]
        mine_out[...] = decode(mine_ref[...]).T.astype(BF16)
        other_out[...] = decode(other_ref[...]).T.astype(BF16)

    out = pl.BlockSpec((BLOCK, tokens), lambda i, place: (i, 0))
    return pl.pallas_call(
        kernel,
        grid_spec=pltpu.PrefetchScalarGridSpec(
            num_scalar_prefetch=1,
            grid=(size // BLOCK,),
            in_specs=[
                pl.BlockSpec((tokens, BLOCK), lambda i, p: (0, lax.rem(p[0], 2) * blocks + first + i)),
                pl.BlockSpec(
                    (tokens, BLOCK), lambda i, p: (0, (1 - lax.rem(p[0], 2)) * blocks + first + i)
                ),
            ]
            + [pl.BlockSpec(memory_space=pl.ANY)] * len(extra),
            out_specs=[out, out],
        ),
        out_shape=[jax.ShapeDtypeStruct((size, tokens), BF16)] * 2,
        compiler_params=pltpu.CompilerParams(vmem_limit_bytes=VMEM),
        cost_estimate=pl.CostEstimate(flops=0, bytes_accessed=20000 * size, transcendentals=0),
        name="decode_act",
    )(place, act_codes, act_codes, *extra)


def decode_grad(place, grad_codes, top, extra):
    tokens, columns = grad_codes.shape
    width = SIDE * COLS

    def kernel(place_ref, code_ref, top_ref, *refs):
        out_refs = refs[len(extra) :]
        for d in range(SIDE):
            target = lax.rem(place_ref[0] + d, SIDE)
            for b in range(2):
                owner = target if b else target + 1 - 2 * lax.rem(target, 2)
                for j in range(SIDE):
                    start = owner * width + lax.rem(place_ref[1] + j, SIDE) * COLS
                    block = decode(code_ref[:, pl.ds(pl.multiple_of(start, COLS), COLS)])
                    out_refs[b * SIDE + d][:, j * COLS : (j + 1) * COLS] = block.astype(BF16)
            filled = jnp.concatenate([top_ref[...]] * (tokens // 8), axis=0)
            out_refs[d][:, width:] = filled.astype(BF16)

    vmem = pl.BlockSpec(memory_space=pltpu.VMEM)
    out = pl.pallas_call(
        kernel,
        in_specs=[pl.BlockSpec(memory_space=pltpu.SMEM), vmem, vmem]
        + [pl.BlockSpec(memory_space=pl.ANY)] * len(extra),
        out_specs=[vmem] * (2 * SIDE),
        out_shape=[jax.ShapeDtypeStruct((tokens, width + TAIL), BF16)] * SIDE
        + [jax.ShapeDtypeStruct((tokens, width), BF16)] * SIDE,
        compiler_params=pltpu.CompilerParams(vmem_limit_bytes=VMEM),
        name="decode_grad",
    )(place, grad_codes, top, *extra)
    return out[:SIDE], out[SIDE:]


def pack(parts, extra):
    def kernel(*refs):
        for r in range(SIDE):
            refs[-1][r] = refs[r][...]

    vmem = pl.BlockSpec(memory_space=pltpu.VMEM)
    return pl.pallas_call(
        kernel,
        in_specs=[vmem] * SIDE + [pl.BlockSpec(memory_space=pl.ANY)] * len(extra),
        out_specs=vmem,
        out_shape=jax.ShapeDtypeStruct((SIDE,) + parts[0].shape, BF16),
        name="pack",
    )(*parts, *extra)


def unjoin(own, joined, size, extra):
    tokens, width = own.shape
    rows, depth = joined[0].shape

    def kernel(own_ref, *refs):
        out_ref = refs[-1]
        out_ref[0] = own_ref[...]
        for r in range(1, SIDE):
            for v in range(width // depth):
                piece = refs[r - 1][v * tokens : (v + 1) * tokens, :]
                out_ref[r, :, v * depth : (v + 1) * depth] = piece

    last = pl.BlockSpec((rows - size, depth), lambda i: (size // (rows - size), 0))
    return pl.pallas_call(
        kernel,
        grid=(1,),
        in_specs=[pl.BlockSpec((tokens, width), lambda i: (0, 0))]
        + [last] * (SIDE - 1)
        + [pl.BlockSpec(memory_space=pl.ANY)] * len(extra),
        out_specs=pl.BlockSpec((SIDE, tokens, width), lambda i: (0, 0, 0)),
        out_shape=jax.ShapeDtypeStruct((SIDE, tokens, width), BF16),
        name="unjoin",
    )(own, *joined, *extra)


def join(acts, grads):
    size, depth = acts[0].shape
    tokens, width = grads[0].shape
    pieces = width // depth

    def kernel(*refs):
        for k in range(len(acts)):
            act_ref, grad_ref, out_ref = refs[k], refs[len(acts) + k], refs[2 * len(acts) + k]
            out_ref[:size, :] = act_ref[...]
            for v in range(pieces):
                at = size + v * tokens
                out_ref[at : at + tokens, :] = grad_ref[:, v * depth : (v + 1) * depth]

    vmem = pl.BlockSpec(memory_space=pltpu.VMEM)
    return pl.pallas_call(
        kernel,
        in_specs=[vmem] * (2 * len(acts)),
        out_specs=[vmem] * len(acts),
        out_shape=[jax.ShapeDtypeStruct((size + pieces * tokens, depth), BF16)] * len(acts),
        compiler_params=pltpu.CompilerParams(vmem_limit_bytes=VMEM),
        name="join",
    )(*acts, *grads)


def scales(gathered):
    groups, _, tokens, columns = gathered.shape

    def kernel(in_ref, scale_ref, inverse_ref):
        found = functools.reduce(
            jnp.maximum, [in_ref[t, r].astype(F32) for t in range(groups) for r in range(SIDE)]
        )
        peak = jnp.full((8, COLS), 1.0, F32) * jnp.max(found)
        scale = jnp.full_like(peak, 2.0**24)
        inverse = jnp.full_like(peak, 2.0**-24)
        for exponent in range(-16, 24):
            above = peak > 2.0**exponent
            scale = jnp.where(above, scale * 0.5, scale)
            inverse = jnp.where(above, inverse * 2.0, inverse)
        scale_ref[...] = scale * (2.0**-10 * NUDGE)
        inverse_ref[...] = inverse

    row = jax.ShapeDtypeStruct((8, COLS), F32)
    out = pl.BlockSpec((8, COLS), lambda i: (0, 0))
    return pl.pallas_call(
        kernel,
        grid=(1,),
        in_specs=[
            pl.BlockSpec((groups, SIDE, 16, TAIL), lambda i: (0, 0, 0, columns // TAIL - 1))
        ],
        out_specs=[out, out],
        out_shape=[row, row],
        name="scales",
    )(gathered)


def two_levels(factor, blocks, size, grads, peak, tokens_after):
    depth = blocks[0].shape[1]
    groups = grads.shape[0]

    def kernel(factor_ref, own_ref, left_ref, right_ref, far_ref, grad_ref, *refs):
        old_ref, out_refs, peak_ref = refs[0], refs[-SIDE - 1 : -1], refs[-1]
        step = pl.program_id(0)

        @pl.when(step == 0)
        def _():
            peak_ref[...] = old_ref[...]

        def tile(out_ref, part):
            rows = pl.ds(part * BLOCK, BLOCK)
            levels = []
            for r, ref in enumerate((own_ref, left_ref, right_ref, far_ref)):
                grad = jnp.concatenate([grad_ref[t, r] for t in range(groups)], axis=0)
                partial = jnp.dot(ref[rows, :], grad, preferred_element_type=F32)
                absolute = jnp.abs(partial)
                pieces = [
                    absolute[8 * u : 8 * u + 8, 128 * v : 128 * v + 128]
                    for u in range(BLOCK // 8)
                    for v in range(COLS // 128)
                ]
                peak_ref[r] = jnp.maximum(peak_ref[r], functools.reduce(jnp.maximum, pieces))
                levels.append(first_level(partial, factor_ref[0:1, :]))
            level = next_level(next_level(levels[0], levels[3]), next_level(levels[1], levels[2]))
            out_ref[rows, :] = level.astype(BF16)

        for d in range(SIDE):

            @pl.when(step == d)
            def _():
                for part in range(size // BLOCK):
                    tile(out_refs[d], part)

    whole = pl.BlockSpec((size, depth), lambda j: (0, 0))
    out = pl.BlockSpec((size, COLS), lambda j: (0, 0))
    small = pl.BlockSpec((SIDE, 8, 128), lambda j: (0, 0, 0))
    *level, peak = pl.pallas_call(
        kernel,
        grid=(SIDE,),
        in_specs=[pl.BlockSpec((8, COLS), lambda j: (0, 0))]
        + [whole] * SIDE
        + [pl.BlockSpec((groups, SIDE, depth // groups, COLS), lambda j: (0, 0, 0, j)), small]
        + [pl.BlockSpec(memory_space=pl.ANY)] * len(tokens_after),
        out_specs=[out] * SIDE + [small],
        out_shape=[jax.ShapeDtypeStruct((size, COLS), BF16)] * SIDE
        + [jax.ShapeDtypeStruct((SIDE, 8, 128), F32)],
        compiler_params=pltpu.CompilerParams(vmem_limit_bytes=VMEM),
        cost_estimate=pl.CostEstimate(
            flops=16 * 10**6 * size, bytes_accessed=7000000, transcendentals=0
        ),
        name="two_levels",
    )(factor, *blocks, grads, peak, *tokens_after)
    return level, peak


def neighbour_levels(own, left, far, right):
    size = own.shape[0]

    def kernel(own_ref, left_ref, far_ref, right_ref, out_ref):
        a, b, c, d = (r[...].astype(F32) for r in (own_ref, far_ref, left_ref, right_ref))
        out_ref[...] = next_level(next_level(a, b), next_level(c, d)).astype(BF16)

    block = pl.BlockSpec((BLOCK, COLS), lambda i: (i, 0))
    return pl.pallas_call(
        kernel,
        grid=(size // BLOCK,),
        in_specs=[block] * 4,
        out_specs=block,
        out_shape=jax.ShapeDtypeStruct((size, COLS), BF16),
        compiler_params=pltpu.CompilerParams(vmem_limit_bytes=VMEM),
        cost_estimate=pl.CostEstimate(flops=0, bytes_accessed=6000000, transcendentals=0),
        name="neighbour_levels",
    )(own, left, far, right)


def last_levels(place, inverse, own, left, far, right, other, start, rows, earlier):
    size = own.shape[0]
    count = size // BLOCK
    blocks = rows // 2 // BLOCK
    first = start // BLOCK

    def kernel(place_ref, inverse_ref, own_ref, left_ref, far_ref, right_ref, other_ref, *refs):
        out_ref = refs[-1]

        @pl.when(pl.program_id(0) == 0)
        def _():
            a, b, c, d = (r[...].astype(F32) for r in (own_ref, far_ref, left_ref, right_ref))
            out_ref[...] = next_level(next_level(a, b), next_level(c, d)) * inverse_ref[0:1, :]

        @pl.when(pl.program_id(0) == 1)
        def _():
            out_ref[...] = other_ref[...].astype(F32) * inverse_ref[0:1, :]

    def out_map(s, i, place):
        side = lax.rem(place[0], 2)
        return (jnp.where(s == 0, side, 1 - side) * blocks + first + i, 0)

    mine = pl.BlockSpec((BLOCK, COLS), lambda s, i, place: (jnp.where(s == 0, i, count - 1), 0))
    extra = [] if earlier is None else [earlier]
    return pl.pallas_call(
        kernel,
        grid_spec=pltpu.PrefetchScalarGridSpec(
            num_scalar_prefetch=1,
            grid=(2, count),
            in_specs=[pl.BlockSpec((8, COLS), lambda s, i, place: (0, 0))]
            + [mine] * 4
            + [pl.BlockSpec((BLOCK, COLS), lambda s, i, place: (jnp.where(s == 1, i, 0), 0))]
            + [pl.BlockSpec(memory_space=pl.ANY)] * len(extra),
            out_specs=pl.BlockSpec((BLOCK, COLS), out_map),
        ),
        out_shape=jax.ShapeDtypeStruct((rows, COLS), F32),
        input_output_aliases={7: 0} if extra else {},
        compiler_params=pltpu.CompilerParams(vmem_limit_bytes=VMEM),
        cost_estimate=pl.CostEstimate(flops=0, bytes_accessed=6000000, transcendentals=0),
        name="last_levels",
    )(place, inverse, own, left, far, right, other, *extra)


def shards(act_codes, grad_codes, amax_history):
    position = lax.axis_index("dp")
    place = jnp.stack([position // SIDE, position % SIDE]).astype(jnp.int32)
    rows = act_codes.shape[1]
    top = jnp.full((8, 128), 1.0, F32) * jnp.max(amax_history)
    top = functools.reduce(jnp.maximum, [along_x(top, d) for d in (2, 1, 3)], top)
    starts = [sum(SIZES[:c]) for c in range(len(SIZES))]
    codes = [decode_act(place, act_codes, starts[c], SIZES[c], []) for c in range(len(SIZES))]
    sent = decode_grad(place, grad_codes, top, [codes[0][0]])

    def arrive(c):
        mine, other = codes[c]
        return (mine, along_y(other, 1), along_y(other, 3), along_y(mine, 2))

    mine, other = codes[0]
    joined = join([other, other, mine], [sent[1][d] for d in (1, 3, 2)])
    parts = [sent[0][0]] + [along_y(sent[0][d], d) for d in (1, 3, 2)]
    grads = [lax.all_gather(pack(parts, joined[:1]), "tensor")]
    factor, inverse = scales(grads[0])
    acts = [(mine,) + tuple(along_y(array, d) for array, d in zip(joined, (1, 3, 2)))]
    parts = unjoin(sent[1][0], acts[0][1:], SIZES[0], [mine for mine, _ in codes])
    grads.append(lax.all_gather(parts, "tensor"))
    acts += [arrive(c) for c in range(1, len(SIZES))]

    peak = jnp.zeros((SIDE, 8, 128), F32)
    levels, sides, done = {}, {}, []
    weight_grad = None
    for c, b, ahead, passed in ORDER:
        extra = list(levels[done[-2]][1:]) if len(done) > 1 else []
        extra += [acts[k][1] for k in ahead] + [sides[k] for k in passed]
        level, peak = two_levels(factor, acts[c], SIZES[c], grads[b], peak, extra)
        levels[c, b] = (level[0], along_x(level[1], 1), along_x(level[2], 2), along_x(level[3], 3))
        done.append((c, b))
        if b == 0:
            sides[c] = swap(neighbour_levels(*levels[c, b]), "dp", SIDE)
        else:
            weight_grad = last_levels(
                place, inverse, *levels[c, b], sides[c], starts[c], rows, weight_grad
            )

    others = (along_y(peak[1], 3), along_y(peak[2], 1), along_y(peak[3], 2))
    current = jnp.max(functools.reduce(jnp.maximum, others, peak[0])) * 2.0**-10
    new_history = jnp.concatenate([current.reshape(1, 1), amax_history[:, :-1]], axis=1)
    return weight_grad, new_history


def solution(mesh):
    return jax.shard_map(
        shards,
        mesh=mesh,
        in_specs=(P("dp", "tensor"), P(("dp", "tensor"), None), P(("dp", "tensor"), None)),
        out_specs=(P("tensor", "dp"), P(("dp", "tensor"), None)),
        check_vma=False,
    )
```
